512 devices in a mesh: shot: 32 (over x, z_lo, core), rcv: 16 (over y, z_hi).
Axes of the slice: x: 4, y: 4, z: 16 (z_hi: 4, z_lo: 4; z = z_hi * 4 + z_lo), core: 2. Of those that a mesh axis runs over, the one named last changes fastest.
Arguments:
- field: bfloat16 [2, 16384, 16384], P(None, 'shot', 'rcv'), may hold values from -1.09375 to 1.09375
Outputs:
- multiples: bfloat16 [2, 16384, 16384], P(None, 'shot', 'rcv')
The draws below stay inside these ranges and needn't reach their ends.
All inputs are finite; a program needn't handle non-finite values.
Results may differ from the reference program's by a relative error of at most 0.001.
Values may be sent and summed in bfloat16 or wider, within the bound.
No kernel may reach another device: no remote copies, remote signals or barrier semaphores. Data moves between devices by JAX's collectives and lax.ppermute only.
A program may use at most 64 MiB of HBM per device.

```python
import math
import jax
import jax.numpy as jnp
from jax import lax

NS = 16384
PANEL = 256
STEPS = 2


def levels(rng, dims, cuts, least, largest):
    level = 1.0
    for axis_at, blocks in cuts:
        heights = jax.random.uniform(jax.random.fold_in(jax.random.fold_in(rng, 6), axis_at), (blocks,), jnp.float32, least / len(cuts), largest / len(cuts))
        level = level * jnp.repeat(jnp.exp(heights), dims[axis_at] // blocks).reshape((-1,) + (1,) * (len(dims) - 1 - axis_at))
    return level


def scatter_about(rng, shape, deviation, bound, shards=(), held_as=jnp.bfloat16):
    values = deviation * jax.random.normal(rng, shape, jnp.float32)
    if shards:
        values = values * levels(rng, shape, shards, -0.22, 0.18)
    return jnp.clip(values, -bound, bound).astype(held_as)


def setup_inputs(seed: int = 0) -> dict:
    splits = jax.random.split(jax.random.key(seed), 2)
    field = scatter_about(splits[0], (2, NS, NS), 0.18, 1.09375, ((1, 32), (2, 16)))
    return dict(field=field)


def reference(field):
    width = STEPS * PANEL
    block = math.gcd(NS, 1024)
    left = field[:, :, :width].reshape(2, NS // block, block, width)
    left = jnp.transpose(left, (1, 0, 2, 3))
    right_real = field[0, :width, :]
    right_imag = field[1, :width, :]

    def one_block(piece):
        real_part = jnp.dot(piece[0], right_real, preferred_element_type=jnp.float32) - jnp.dot(piece[1], right_imag, preferred_element_type=jnp.float32)
        imag_part = jnp.dot(piece[0], right_imag, preferred_element_type=jnp.float32) + jnp.dot(piece[1], right_real, preferred_element_type=jnp.float32)
        return jnp.stack([-real_part, -imag_part]).astype(jnp.bfloat16)

    result = lax.map(one_block, left)
    return jnp.transpose(result, (1, 0, 2, 3)).reshape(2, NS, NS)
```

```python
import jax
import jax.numpy as jnp
from jax import lax
from jax.sharding import PartitionSpec as P

WIDTH = 512
AXES = ("shot", "rcv")
NX, NL, NC, NY, NH = 4, 4, 2, 4, 4


def moves(rule):
    pairs = []
    for x in range(NX):
        for l in range(NL):
            for c in range(NC):
                for y in range(NY):
                    for h in range(NH):
                        to = rule(x, l, c, y, h)
                        if to is None:
                            continue
                        X, L, C, Y, H = to
                        src = ((x * NL + l) * NC + c) * NY * NH + y * NH + h
                        dst = (((X % NX) * NL + L) * NC + C) * NY * NH + (Y % NY) * NH + H % NH
                        pairs.append((src, dst))
    return pairs


def send(value, rule):
    return lax.ppermute(value, AXES, moves(rule))


def place(whole, piece, index):
    return lax.dynamic_update_slice_in_dim(whole, piece, index * piece.shape[1], 1)


def left_panel(field, x, l, c, y, h):
    mine = field[:, :, :WIDTH]
    rows = mine.shape[1]
    part = rows // NY
    got = [
        send(mine[:, part * d : part * (d + 1)], lambda x, l, c, y, h, d=d: (x, l, c, d, h) if y == 0 and h == 0 else None)
        for d in (1, 3, 2)
    ]
    quarter = jnp.where(y == 0, mine[:, :part], got[0] + got[1] + got[2])
    bit = part // NH
    got = [
        send(quarter[:, bit * d : bit * (d + 1)], lambda x, l, c, y, h, d=d: (x, l, c, y, d) if h == 0 else None)
        for d in (1, 3, 2)
    ]
    own = jnp.where(h == 0, quarter[:, :bit], got[0] + got[1] + got[2])
    gathered = place(quarter, own, h)
    for d in (1, 3, 2):
        came = send(own, lambda x, l, c, y, h, d=d: (x, l, c, y, h + d) if (h + d) % NH != 0 else None)
        gathered = place(gathered, came, (h - d) % NH)
    quarter = jnp.where(h == 0, quarter, gathered)
    panel = place(mine, quarter, y)
    for d in (1, 3, 2):
        came = send(quarter, lambda x, l, c, y, h, d=d: (x, l, c, y + d, h))
        panel = place(panel, came, (y - d) % NY)
    return panel


def right_panel(field, x, l, c, y, h):
    mine = field[:, :WIDTH, :]
    part = WIDTH // NX
    got = [
        send(mine[:, part * d : part * (d + 1)], lambda x, l, c, y, h, d=d: (d, l, c, y, h) if x == 0 and l == 0 and c == 0 else None)
        for d in (1, 3, 2)
    ]
    quarter = jnp.where(x == 0, mine[:, :part], got[0] + got[1] + got[2])
    came = send(quarter, lambda x, l, c, y, h: (x, 2, c, y, h) if l == 0 and c == 0 else None)
    quarter = jnp.where(l == 2, came, quarter)
    came = send(quarter, lambda x, l, c, y, h: (x, l + 1, c, y, h) if l % 2 == 0 and c == 0 else None)
    quarter = jnp.where(l % 2 == 1, came, quarter)
    panel = place(mine, quarter, x)
    for d in (1, 3, 2):
        came = send(quarter, lambda x, l, c, y, h, d=d: (x + d, l, c, y, h) if c == 0 else None)
        panel = place(panel, came, (x - d) % NX)
    came = send(panel, lambda x, l, c, y, h: (x, l, 1, y, h) if c == 0 else None)
    return jnp.where(c == 0, panel, came)


def per_device(field):
    s, r = lax.axis_index("shot"), lax.axis_index("rcv")
    place_of = (s // (NL * NC), s // NC % NL, s % NC, r // NH, r % NH)
    left = left_panel(field, *place_of)
    right = right_panel(field, *place_of)
    dot = lambda a, b: jnp.dot(a, b, preferred_element_type=jnp.float32)
    real = dot(left[0], right[0]) - dot(left[1], right[1])
    imag = dot(left[0], right[1]) + dot(left[1], right[0])
    return jnp.stack([-real, -imag]).astype(jnp.bfloat16)


def solution(mesh):
    return jax.shard_map(
        per_device,
        mesh=mesh,
        in_specs=(P(None, "shot", "rcv"),),
        out_specs=P(None, "shot", "rcv"),
        check_vma=False,
    )
```

```python
import jax
import jax.numpy as jnp
from jax import lax
from jax.sharding import PartitionSpec as P

WIDTH = 512
AXES = ("shot", "rcv")
NX, NL, NC, NY, NH = 4, 4, 2, 4, 4
HOPS = (2, 1, 3)


def moves(rule):
    pairs = []
    for x in range(NX):
        for l in range(NL):
            for c in range(NC):
                for y in range(NY):
                    for h in range(NH):
                        to = rule(x, l, c, y, h)
                        if to is None:
                            continue
                        X, L, C, Y, H = to
                        src = ((x * NL + l) * NC + c) * NY * NH + y * NH + h
                        dst = (((X % NX) * NL + L) * NC + C) * NY * NH + (Y % NY) * NH + H % NH
                        pairs.append((src, dst))
    return pairs


def send(value, rule):
    return lax.ppermute(value, AXES, moves(rule))


def place(whole, piece, index):
    return lax.dynamic_update_slice_in_dim(whole, piece, index * piece.shape[1], 1)


def after(value, *others):
    return lax.optimization_barrier((value, *others))[0]


def per_device(field):
    s, r = lax.axis_index("shot"), lax.axis_index("rcv")
    x, l, c, y, h = s // (NL * NC), s // NC % NL, s % NC, r // NH, r % NH

    lmine = field[:, :, :WIDTH]
    rmine = field[:, :WIDTH]
    half = rmine.shape[2] // NC
    lpart = lmine.shape[1] // NY
    rpart = WIDTH // NX

    rhalf1 = send(rmine[:, :, half:], lambda x, l, c, y, h: (x, l, 1, y, h) if x == 0 and l == 0 and c == 0 else None)

    lgot = {
        d: send(lmine[:, lpart * d : lpart * (d + 1)], lambda x, l, c, y, h, d=d: (x, l, c, d, h) if y == 0 and h == 0 else None)
        for d in HOPS
    }
    rhalf = jnp.where(c == 0, rmine[:, :, :half], rhalf1)
    rgot = {
        d: send(rhalf[:, rpart * d : rpart * (d + 1)], lambda x, l, c, y, h, d=d: (d, l, c, y, h) if x == 0 and l == 0 else None)
        for d in HOPS
    }
    lq = jnp.where(y == 0, lmine[:, :lpart], lgot[1] + lgot[2] + lgot[3])

    bit = lpart // 8
    a, b, e = slice(0, 3 * bit), slice(3 * bit, 5 * bit), slice(5 * bit, 8 * bit)
    z1 = {
        d: send(lq[:, w], lambda x, l, c, y, h, d=d: (x, l, c, y, d) if h == 0 else None)
        for d, w in ((1, a), (3, e), (2, b))
    }
    rq = jnp.where(x == 0, rhalf[:, :rpart], rgot[1] + rgot[2] + rgot[3])
    rq = after(rq, lq)
    came = send(rq, lambda x, l, c, y, h: (x, 2, c, y, h) if l == 0 else None)

    wide = jnp.concatenate([z1[2], jnp.zeros_like(z1[2][:, : 3 * bit - 2 * bit])], 1)
    up = jnp.where(h == 0, lq[:, e], jnp.where(h == 1, z1[1], wide))
    down = jnp.where(h == 0, lq[:, a], jnp.where(h == 3, z1[3], wide))
    gup = send(up, lambda x, l, c, y, h: (x, l, c, y, h + 1) if h < 3 else None)
    gdown = send(down, lambda x, l, c, y, h: (x, l, c, y, h - 1) if h != 1 else None)
    rq = jnp.where(l == 2, came, rq)
    rq = after(rq, up, down)
    came = send(rq, lambda x, l, c, y, h: (x, l + 1, c, y, h) if l % 2 == 0 else None)
    rq = jnp.where(l % 2 == 1, came, rq)

    right = jnp.zeros((2, WIDTH, half), jnp.bfloat16)
    right = place(right, rq, x)
    for d in HOPS:
        came = send(rq, lambda x, l, c, y, h, d=d: (x + d, l, c, y, h))
        right = place(right, came, (x - d) % NX)
    other = send(right, lambda x, l, c, y, h: (x, l, 1 - c, y, h))

    pa = jnp.where(h == 1, z1[1], jnp.where(h == 2, gup, gdown))
    pb = jnp.where(h == 2, z1[2], jnp.where(h == 1, gdown, gup)[:, : 2 * bit])
    pe = jnp.where(h == 3, z1[3], jnp.where(h == 1, gup, gdown))
    lq = jnp.where(h == 0, lq, jnp.concatenate([pa, pb, pe], 1))
    left = jnp.zeros_like(lmine)
    left = place(left, lq, y)
    for d in HOPS:
        came = send(lq, lambda x, l, c, y, h, d=d: (x, l, c, y + d, h))
        left = place(left, came, (y - d) % NY)

    right = jnp.where(c == 0, jnp.concatenate([right, other], 2), jnp.concatenate([other, right], 2))
    dot = lambda a, b: jnp.dot(a, b, preferred_element_type=jnp.float32)
    real = dot(left[0], right[0]) - dot(left[1], right[1])
    imag = dot(left[0], right[1]) + dot(left[1], right[0])
    return jnp.stack([-real, -imag]).astype(jnp.bfloat16)


def solution(mesh):
    return jax.shard_map(
        per_device,
        mesh=mesh,
        in_specs=(P(None, "shot", "rcv"),),
        out_specs=P(None, "shot", "rcv"),
        check_vma=False,
    )
```

```python
import jax
import jax.numpy as jnp
from jax import lax
from jax.experimental import pallas as pl
from jax.experimental.pallas import tpu as pltpu
from jax.sharding import PartitionSpec as P

WIDTH = 512
AXES = ("shot", "rcv")
NX, NL, NC, NY, NH = 4, 4, 2, 4, 4
VMEM = pl.BlockSpec(memory_space=pltpu.VMEM)
SMEM = pl.BlockSpec(memory_space=pltpu.SMEM)
HBM = pl.BlockSpec(memory_space=pl.ANY)


def moves(rule):
    pairs = []
    for x in range(NX):
        for l in range(NL):
            for c in range(NC):
                for y in range(NY):
                    for h in range(NH):
                        to = rule(x, l, c, y, h)
                        if to is None:
                            continue
                        X, L, C, Y, H = to
                        src = ((x * NL + l) * NC + c) * NY * NH + y * NH + h
                        dst = (((X % NX) * NL + L) * NC + C) * NY * NH + (Y % NY) * NH + H % NH
                        pairs.append((src, dst))
    return pairs


def send(value, rule):
    return lax.ppermute(value, AXES, moves(rule))


def pick(index, choices):
    out = choices[-1]
    for i, choice in enumerate(choices[:-1]):
        out = jnp.where(index == i, choice, out)
    return out


def cut_kernel(role, field, came, *refs):
    units, sem = refs[:-1], refs[-1]
    rows = units[0].shape[1]
    cols = units[0].shape[2]

    def run(copies):
        for copy in copies:
            copy.start()
        for copy in copies:
            copy.wait()

    @pl.when(role[0] == 1)
    def _():
        run([
            pltpu.make_async_copy(
                field.at[:, pl.ds(rows * d, rows), pl.ds(cols * t, cols)], unit.at[pl.ds(2 * t, 2)], sem.at[2 * d + t]
            )
            for d, unit in enumerate(units)
            for t in range(2)
        ])

    @pl.when(role[0] == 2)
    def _():
        run([
            pltpu.make_async_copy(
                came.at[:, pl.ds(rows * d, rows)] if t == 0 else field.at[:, pl.ds(rows * d, rows), pl.ds(0, cols)],
                unit.at[pl.ds(2 * t, 2)],
                sem.at[2 * d + t],
            )
            for d, unit in enumerate(units)
            for t in range(2)
        ])


def cut(role, field, came, unit_shape):
    return pl.pallas_call(
        cut_kernel,
        out_shape=[jax.ShapeDtypeStruct(unit_shape, jnp.bfloat16)] * 4,
        in_specs=[SMEM, HBM, HBM],
        out_specs=[VMEM] * 4,
        scratch_shapes=[pltpu.SemaphoreType.DMA((8,))],
        compiler_params=pltpu.CompilerParams(vmem_limit_bytes=16 * 1024 * 1024),
    )(role, field, came)


def product_kernel(at, *refs):
    mine, theirs = refs[0:4], refs[4:8]
    out, lre, lim, buf, sem = refs[8:]
    rows = mine[0].shape[1]
    dot = lambda a, b: jnp.dot(a, b, preferred_element_type=jnp.float32)

    def work(lefts, rights, first):
        for i, left in enumerate(lefts):
            for j in range(4):
                k = pl.ds(pl.multiple_of(at[5 + j], rows), rows)
                re, im = left[first, :, k], left[first + 1, :, k]
                here = pl.ds(rows * i, rows)
                lre[j, here, :rows] = -re
                lre[j, here, rows:] = im
                lim[j, here, :rows] = -im
                lim[j, here, rows:] = -re
        copies = []
        for i in range(4):
            here = pl.ds(rows * i, rows)
            for t in range(2):
                cols = pl.ds(WIDTH * t, WIDTH)
                for q, lhs in ((0, lre), (1, lim)):
                    acc = None
                    for j, right in enumerate(rights):
                        both = right[2 * t : 2 * t + 2].reshape(2 * rows, WIDTH)
                        term = dot(lhs[j, here], both)
                        acc = term if acc is None else acc + term
                    buf[i, q, :, cols] = acc.astype(buf.dtype)
            place = pl.ds(pl.multiple_of(at[1 + i], rows), rows)
            copies.append(pltpu.make_async_copy(buf.at[i], out.at[:, place], sem.at[i]))
            copies[-1].start()
        for copy in copies:
            copy.wait()

    @pl.when(at[0] == 0)
    def _():
        work(theirs, mine, 0)

    @pl.when(at[0] == 1)
    def _():
        work(mine, theirs, 2)


def product(at, mine, theirs, shape):
    rows = mine[0].shape[1]
    return pl.pallas_call(
        product_kernel,
        out_shape=jax.ShapeDtypeStruct(shape, jnp.bfloat16),
        in_specs=[SMEM] + [VMEM] * 8,
        out_specs=HBM,
        scratch_shapes=[
            pltpu.VMEM((4, 4 * rows, 2 * rows), jnp.bfloat16),
            pltpu.VMEM((4, 4 * rows, 2 * rows), jnp.bfloat16),
            pltpu.VMEM((4, 2, rows, shape[2]), jnp.bfloat16),
            pltpu.SemaphoreType.DMA((4,)),
        ],
        compiler_params=pltpu.CompilerParams(vmem_limit_bytes=40 * 1024 * 1024),
        cost_estimate=pl.CostEstimate(flops=8 * shape[1] * shape[2] * WIDTH, bytes_accessed=1 << 22, transcendentals=0),
    )(at, *mine, *theirs)


def per_device(field):
    s, r = lax.axis_index("shot"), lax.axis_index("rcv")
    x, l, c, y, h = s // (NL * NC), s // NC % NL, s % NC, r // NH, r % NH
    part = WIDTH // 4
    unit_shape = (4, part, WIDTH)

    came = send(field[:, :, :WIDTH], lambda x, l, c, y, h: (x, l, 1, y, h) if c == 0 and y == 0 and h == 0 else None)
    right_root = (c == 0) & (x == 0) & (l == 0)
    left_root = (c == 1) & (y == 0) & (h == 0)
    role = jnp.where(right_root, 1, jnp.where(left_root, 2, 0)).astype(jnp.int32).reshape(1)
    units = cut(role, field, came, unit_shape)

    def scatter(d):
        def rule(x, l, c, y, h):
            if c == 0:
                return (d, l, c, y, h) if x == 0 and l == 0 else None
            return (x, l, c, d, h) if y == 0 and h == 0 else None
        return rule

    got = {d: send(units[d], scatter(d)) for d in (2, 1, 3)}
    unit = jnp.where(jnp.where(c == 0, x, y) == 0, units[0], got[1] + got[2] + got[3])

    a, e = unit[:, : part // 2], unit[:, part // 2 :]

    def hop(to):
        def rule(x, l, c, y, h):
            if c == 0:
                return (x, 2, c, y, h) if l == 0 else None
            return (x, l, c, y, to) if h == 0 else None
        return rule

    za, ze = lax.optimization_barrier((send(a, hop(1)), send(e, hop(3))))

    def onwards(step, sources):
        def rule(x, l, c, y, h):
            if c == 0:
                return (x, l + 1, c, y, h) if l in (0, 2) else None
            return (x, l, c, y, h + step) if h in sources else None
        return rule

    start = jnp.where(c == 0, l, h) == 0
    up = jnp.where(start, jnp.where(c == 0, a, e), za)
    down = jnp.where(start, jnp.where(c == 0, e, a), ze)
    up, down = lax.optimization_barrier((up, down))
    gup, gdown = send(up, onwards(1, (0, 1))), send(down, onwards(-1, (0, 3)))
    a_from = jnp.where(c == 0, pick(l, (0, 2, 1, 2)), pick(h, (0, 1, 2, 3)))
    e_from = jnp.where(c == 0, pick(l, (0, 3, 1, 3)), pick(h, (0, 2, 3, 1)))
    unit = jnp.concatenate([pick(a_from, (a, za, gup, gdown)), pick(e_from, (e, ze, gup, gdown))], 1)

    def gather(d):
        return lambda x, l, c, y, h: (x + d, l, c, y, h) if c == 0 else (x, l, c, y + d, h)

    order = (0, 2, 1, 3)
    mine = [unit] + [send(unit, gather(d)) for d in order[1:]]
    theirs = [send(value, lambda x, l, c, y, h: (x, l, 1 - c, y, h)) for value in mine]
    at = jnp.stack([c] + [(y - d) % NY * part for d in order] + [(x - d) % NX * part for d in order]).astype(jnp.int32)
    return product(at, mine, theirs, field.shape)


def solution(mesh):
    return jax.shard_map(
        per_device,
        mesh=mesh,
        in_specs=(P(None, "shot", "rcv"),),
        out_specs=P(None, "shot", "rcv"),
        check_vma=False,
    )
```

```python
import jax
import jax.numpy as jnp
from jax import lax
from jax.experimental import pallas as pl
from jax.experimental.pallas import tpu as pltpu
from jax.sharding import PartitionSpec as P

WIDTH = 512
AXES = ("shot", "rcv")
NX, NL, NC, NY, NH = 4, 4, 2, 4, 4
VMEM = pl.BlockSpec(memory_space=pltpu.VMEM)
SMEM = pl.BlockSpec(memory_space=pltpu.SMEM)
HBM = pl.BlockSpec(memory_space=pltpu.HBM)


def moves(rule):
    pairs = []
    for x in range(NX):
        for l in range(NL):
            for c in range(NC):
                for y in range(NY):
                    for h in range(NH):
                        to = rule(x, l, c, y, h)
                        if to is None:
                            continue
                        X, L, C, Y, H = to
                        src = ((x * NL + l) * NC + c) * NY * NH + y * NH + h
                        dst = (((X % NX) * NL + L) * NC + C) * NY * NH + (Y % NY) * NH + H % NH
                        pairs.append((src, dst))
    return pairs


def send(value, rule):
    return lax.ppermute(value, AXES, moves(rule))


def pick(index, choices):
    out = choices[-1]
    for i, choice in enumerate(choices[:-1]):
        out = jnp.where(index == i, choice, out)
    return out


def run(copies):
    for copy in copies:
        copy.start()
    for copy in copies:
        copy.wait()


def first_kernel(role, field, *refs):
    panel, bits, sem = refs[0], refs[1:-1], refs[-1]
    rows = bits[0].shape[1]
    cols = bits[0].shape[2]

    @pl.when(role[0] == 1)
    def _():
        run([
            pltpu.make_async_copy(
                field.at[:, pl.ds(rows * i, rows), pl.ds(cols * t, cols)], bit.at[pl.ds(2 * t, 2)], sem.at[2 * i + t]
            )
            for i, bit in enumerate(bits)
            for t in range(2)
        ])

    @pl.when(role[1] == 1)
    def _():
        run([pltpu.make_async_copy(field.at[:, :, pl.ds(0, cols)], panel, sem.at[16])])


def first(role, field, shape):
    return pl.pallas_call(
        first_kernel,
        out_shape=[jax.ShapeDtypeStruct((2, field.shape[1], WIDTH), jnp.bfloat16)]
        + [jax.ShapeDtypeStruct(shape, jnp.bfloat16)] * 8,
        in_specs=[SMEM, HBM],
        out_specs=[VMEM] * 9,
        scratch_shapes=[pltpu.SemaphoreType.DMA((17,))],
        compiler_params=pltpu.CompilerParams(vmem_limit_bytes=16 * 1024 * 1024),
    )(role, field)


def second_kernel(role, field, came, *refs):
    bits, sem = refs[8:-1], refs[-1]
    rows = bits[0].shape[1]
    cols = bits[0].shape[2]

    @pl.when(role[2] == 1)
    def _():
        run([
            pltpu.make_async_copy(
                came.at[:, pl.ds(rows * i, rows)] if t == 0 else field.at[:, pl.ds(rows * i, rows), pl.ds(0, cols)],
                bit.at[pl.ds(2 * t, 2)],
                sem.at[2 * i + t],
            )
            for i, bit in enumerate(bits)
            for t in range(2)
        ])


def second(role, field, came, bits):
    return pl.pallas_call(
        second_kernel,
        out_shape=[jax.ShapeDtypeStruct(bit.shape, bit.dtype) for bit in bits],
        in_specs=[SMEM, HBM] + [VMEM] * 9,
        out_specs=[VMEM] * 8,
        input_output_aliases={3 + i: i for i in range(8)},
        scratch_shapes=[pltpu.SemaphoreType.DMA((16,))],
        compiler_params=pltpu.CompilerParams(vmem_limit_bytes=16 * 1024 * 1024),
    )(role, field, came, *bits)


def product_kernel(at, *refs):
    mine, theirs = refs[0:4], refs[4:8]
    out, lre, lim, buf, sem = refs[8:]
    rows = mine[0].shape[1]
    dot = lambda a, b: jnp.dot(a, b, preferred_element_type=jnp.float32)

    def work(lefts, rights, first):
        for i, left in enumerate(lefts):
            for j in range(4):
                k = pl.ds(pl.multiple_of(at[5 + j], rows), rows)
                re, im = left[first, :, k], left[first + 1, :, k]
                here = pl.ds(rows * i, rows)
                lre[j, here, :rows] = -re
                lre[j, here, rows:] = im
                lim[j, here, :rows] = -im
                lim[j, here, rows:] = -re
        copies = []
        for i in range(4):
            here = pl.ds(rows * i, rows)
            for t in range(2):
                cols = pl.ds(WIDTH * t, WIDTH)
                for q, lhs in ((0, lre), (1, lim)):
                    acc = None
                    for j, right in enumerate(rights):
                        both = right[2 * t : 2 * t + 2].reshape(2 * rows, WIDTH)
                        term = dot(lhs[j, here], both)
                        acc = term if acc is None else acc + term
                    buf[i, q, :, cols] = acc.astype(buf.dtype)
            place = pl.ds(pl.multiple_of(at[1 + i], rows), rows)
            copies.append(pltpu.make_async_copy(buf.at[i], out.at[:, place], sem.at[i]))
            copies[-1].start()
        for copy in copies:
            copy.wait()

    @pl.when(at[0] == 0)
    def _():
        work(theirs, mine, 0)

    @pl.when(at[0] == 1)
    def _():
        work(mine, theirs, 2)


def product(at, mine, theirs, shape):
    rows = mine[0].shape[1]
    return pl.pallas_call(
        product_kernel,
        out_shape=jax.ShapeDtypeStruct(shape, jnp.bfloat16),
        in_specs=[SMEM] + [VMEM] * 8,
        out_specs=HBM,
        scratch_shapes=[
            pltpu.VMEM((4, 4 * rows, 2 * rows), jnp.bfloat16),
            pltpu.VMEM((4, 4 * rows, 2 * rows), jnp.bfloat16),
            pltpu.VMEM((4, 2, rows, shape[2]), jnp.bfloat16),
            pltpu.SemaphoreType.DMA((4,)),
        ],
        compiler_params=pltpu.CompilerParams(vmem_limit_bytes=40 * 1024 * 1024),
        cost_estimate=pl.CostEstimate(flops=8 * shape[1] * shape[2] * WIDTH, bytes_accessed=1 << 22, transcendentals=0),
    )(at, *mine, *theirs)


def per_device(field):
    s, r = lax.axis_index("shot"), lax.axis_index("rcv")
    x, l, c, y, h = s // (NL * NC), s // NC % NL, s % NC, r // NH, r % NH
    part = WIDTH // 4

    left_root = (y == 0) & (h == 0)
    role = jnp.stack([(c == 0) & (x == 0) & (l == 0), left_root & (c == 0), left_root & (c == 1)]).astype(jnp.int32)
    panel, *bits = first(role, field, (4, part // 2, WIDTH))
    came = send(panel, lambda x, l, c, y, h: (x, l, 1, y, h) if c == 0 and y == 0 and h == 0 else None)
    bits = second(role, field, came, bits)

    def scatter(d):
        def rule(x, l, c, y, h):
            if c == 0:
                return (d, l, c, y, h) if x == 0 and l == 0 else None
            return (x, l, c, d, h) if y == 0 and h == 0 else None
        return rule

    at_root = jnp.where(c == 0, x, y) == 0
    a, e = (
        jnp.where(at_root, bits[t], sum(send(bits[2 * d + t], scatter(d)) for d in (1, 3, 2)))
        for t in range(2)
    )


    def hop(to):
        def rule(x, l, c, y, h):
            if c == 0:
                return (x, 2, c, y, h) if l == 0 else None
            return (x, l, c, y, to) if h == 0 else None
        return rule

    za, ze = lax.optimization_barrier((send(a, hop(1)), send(e, hop(3))))

    def onwards(step, sources):
        def rule(x, l, c, y, h):
            if c == 0:
                return (x, l + 1, c, y, h) if l in (0, 2) else None
            return (x, l, c, y, h + step) if h in sources else None
        return rule

    start = jnp.where(c == 0, l, h) == 0
    up = jnp.where(start, jnp.where(c == 0, a, e), za)
    down = jnp.where(start, jnp.where(c == 0, e, a), ze)
    up, down = lax.optimization_barrier((up, down))
    gup, gdown = send(up, onwards(1, (0, 1))), send(down, onwards(-1, (0, 3)))
    a_from = jnp.where(c == 0, pick(l, (0, 2, 1, 2)), pick(h, (0, 1, 2, 3)))
    e_from = jnp.where(c == 0, pick(l, (0, 3, 1, 3)), pick(h, (0, 2, 3, 1)))
    unit = jnp.concatenate([pick(a_from, (a, za, gup, gdown)), pick(e_from, (e, ze, gup, gdown))], 1)

    def gather(d):
        return lambda x, l, c, y, h: (x + d, l, c, y, h) if c == 0 else (x, l, c, y + d, h)

    order = (0, 1, 3, 2)
    mine = [unit] + [send(unit, gather(d)) for d in order[1:]]
    theirs = [send(value, lambda x, l, c, y, h: (x, l, 1 - c, y, h)) for value in mine]
    at = jnp.stack([c] + [(y - d) % NY * part for d in order] + [(x - d) % NX * part for d in order]).astype(jnp.int32)
    return product(at, mine, theirs, field.shape)


def solution(mesh):
    return jax.shard_map(
        per_device,
        mesh=mesh,
        in_specs=(P(None, "shot", "rcv"),),
        out_specs=P(None, "shot", "rcv"),
        check_vma=False,
    )
```

```python
import jax
import jax.numpy as jnp
from jax import lax
from jax.experimental import pallas as pl
from jax.experimental.pallas import tpu as pltpu
from jax.sharding import PartitionSpec as P

WIDTH = 512
AXES = ("shot", "rcv")
NX, NL, NC, NY, NH = 4, 4, 2, 4, 4
VMEM = pl.BlockSpec(memory_space=pltpu.VMEM)
SMEM = pl.BlockSpec(memory_space=pltpu.SMEM)
HBM = pl.BlockSpec(memory_space=pltpu.HBM)


def moves(rule):
    pairs = []
    for x in range(NX):
        for l in range(NL):
            for c in range(NC):
                for y in range(NY):
                    for h in range(NH):
                        to = rule(x, l, c, y, h)
                        if to is None:
                            continue
                        X, L, C, Y, H = to
                        src = ((x * NL + l) * NC + c) * NY * NH + y * NH + h
                        dst = (((X % NX) * NL + L) * NC + C) * NY * NH + (Y % NY) * NH + H % NH
                        pairs.append((src, dst))
    return pairs


def send(value, rule):
    return lax.ppermute(value, AXES, moves(rule))


def pick(index, choices):
    out = choices[-1]
    for i, choice in enumerate(choices[:-1]):
        out = jnp.where(index == i, choice, out)
    return out


def run(copies):
    for copy in copies:
        copy.start()
    for copy in copies:
        copy.wait()


def first_kernel(role, field, *refs):
    panel, upper, lower, sem = refs[0], refs[1:5], refs[5:9], refs[9]
    rows, cols = upper[0].shape[1:]

    def part(d, t):
        return field.at[:, pl.ds(rows * d, rows), pl.ds(cols * t, cols)]

    @pl.when(role[0] == 1)
    def _():
        run([
            pltpu.make_async_copy(part(d, t), bits[d], sem.at[2 * d + t])
            for d in range(4)
            for t, bits in ((1, upper), (0, lower))
        ])

    @pl.when(role[1] == 1)
    def _():
        run([pltpu.make_async_copy(field.at[:, :, pl.ds(0, cols)], panel, sem.at[8])])

    @pl.when(role[2] == 1)
    def _():
        run([pltpu.make_async_copy(part(d, 0), bit, sem.at[d]) for d, bit in enumerate(upper)])


def first(role, field, shape):
    return pl.pallas_call(
        first_kernel,
        out_shape=[jax.ShapeDtypeStruct((2, field.shape[1], WIDTH), jnp.bfloat16)]
        + [jax.ShapeDtypeStruct(shape, jnp.bfloat16)] * 8,
        in_specs=[SMEM, HBM],
        out_specs=[VMEM] * 9,
        scratch_shapes=[pltpu.SemaphoreType.DMA((9,))],
        compiler_params=pltpu.CompilerParams(vmem_limit_bytes=16 * 1024 * 1024),
    )(role, field)


def second_kernel(role, came, *refs):
    lower, sem = refs[4:8], refs[8]
    rows = lower[0].shape[1]

    @pl.when(role[2] == 1)
    def _():
        run([
            pltpu.make_async_copy(came.at[:, pl.ds(rows * d, rows)], bit, sem.at[d]) for d, bit in enumerate(lower)
        ])


def second(role, came, bits):
    return pl.pallas_call(
        second_kernel,
        out_shape=[jax.ShapeDtypeStruct(bit.shape, bit.dtype) for bit in bits],
        in_specs=[SMEM] + [VMEM] * 5,
        out_specs=[VMEM] * 4,
        input_output_aliases={2 + i: i for i in range(4)},
        scratch_shapes=[pltpu.SemaphoreType.DMA((4,))],
        compiler_params=pltpu.CompilerParams(vmem_limit_bytes=16 * 1024 * 1024),
    )(role, came, *bits)


def product_kernel(at, *refs):
    mine, theirs = refs[0:4], refs[4:8]
    out, lre, lim, buf, sem = refs[8:]
    rows = mine[0].shape[1]
    dot = lambda a, b: jnp.dot(a, b, preferred_element_type=jnp.float32)

    def work(lefts, rights, first):
        for i, left in enumerate(lefts):
            for j in range(4):
                k = pl.ds(pl.multiple_of(at[5 + j], rows), rows)
                re, im = left[first, :, k], left[first + 1, :, k]
                here = pl.ds(rows * i, rows)
                lre[j, here, :rows] = -re
                lre[j, here, rows:] = im
                lim[j, here, :rows] = -im
                lim[j, here, rows:] = -re
        copies = []
        for i in range(4):
            here = pl.ds(rows * i, rows)
            for t in range(2):
                cols = pl.ds(WIDTH * t, WIDTH)
                for q, lhs in ((0, lre), (1, lim)):
                    acc = None
                    for j, right in enumerate(rights):
                        both = right[2 * t : 2 * t + 2].reshape(2 * rows, WIDTH)
                        term = dot(lhs[j, here], both)
                        acc = term if acc is None else acc + term
                    buf[i, q, :, cols] = acc.astype(buf.dtype)
            place = pl.ds(pl.multiple_of(at[1 + i], rows), rows)
            copies.append(pltpu.make_async_copy(buf.at[i], out.at[:, place], sem.at[i]))
            copies[-1].start()
        for copy in copies:
            copy.wait()

    @pl.when(at[0] == 0)
    def _():
        work(theirs, mine, 0)

    @pl.when(at[0] == 1)
    def _():
        work(mine, theirs, 2)


def product(at, mine, theirs, shape):
    rows = mine[0].shape[1]
    return pl.pallas_call(
        product_kernel,
        out_shape=jax.ShapeDtypeStruct(shape, jnp.bfloat16),
        in_specs=[SMEM] + [VMEM] * 8,
        out_specs=HBM,
        scratch_shapes=[
            pltpu.VMEM((4, 4 * rows, 2 * rows), jnp.bfloat16),
            pltpu.VMEM((4, 4 * rows, 2 * rows), jnp.bfloat16),
            pltpu.VMEM((4, 2, rows, shape[2]), jnp.bfloat16),
            pltpu.SemaphoreType.DMA((4,)),
        ],
        compiler_params=pltpu.CompilerParams(vmem_limit_bytes=40 * 1024 * 1024),
        cost_estimate=pl.CostEstimate(flops=8 * shape[1] * shape[2] * WIDTH, bytes_accessed=1 << 22, transcendentals=0),
    )(at, *mine, *theirs)


def per_device(field):
    s, r = lax.axis_index("shot"), lax.axis_index("rcv")
    x, l, c, y, h = s // (NL * NC), s // NC % NL, s % NC, r // NH, r % NH
    part = WIDTH // 4

    left_root = (y == 0) & (h == 0)
    role = jnp.stack([(c == 0) & (x == 0) & (l == 0), left_root & (c == 0), left_root & (c == 1)]).astype(jnp.int32)
    panel, *bits = first(role, field, (2, part, WIDTH))
    upper, lower = bits[:4], bits[4:]
    came = send(panel, lambda x, l, c, y, h: (x, l, 1, y, h) if c == 0 and y == 0 and h == 0 else None)
    lower = second(role, came, lower)

    def scatter(d):
        def rule(x, l, c, y, h):
            if c == 0:
                return (d, l, c, y, h) if x == 0 and l == 0 else None
            return (x, l, c, d, h) if y == 0 and h == 0 else None
        return rule

    at_root = jnp.where(c == 0, x, y) == 0
    a, e = (
        jnp.where(at_root, bits[0], sum(send(bits[d], scatter(d)) for d in (1, 3, 2)))
        for bits in (upper, lower)
    )


    def hop(to):
        def rule(x, l, c, y, h):
            if c == 0:
                return (x, 2, c, y, h) if l == 0 else None
            return (x, l, c, y, to) if h == 0 else None
        return rule

    za, ze = lax.optimization_barrier((send(a, hop(1)), send(e, hop(3))))

    def onwards(step, sources):
        def rule(x, l, c, y, h):
            if c == 0:
                return (x, l + 1, c, y, h) if l in (0, 2) else None
            return (x, l, c, y, h + step) if h in sources else None
        return rule

    start = jnp.where(c == 0, l, h) == 0
    up = jnp.where(start, jnp.where(c == 0, a, e), za)
    down = jnp.where(start, jnp.where(c == 0, e, a), ze)
    up, down = lax.optimization_barrier((up, down))
    gup, gdown = send(up, onwards(1, (0, 1))), send(down, onwards(-1, (0, 3)))
    a_from = jnp.where(c == 0, pick(l, (0, 2, 1, 2)), pick(h, (0, 1, 2, 3)))
    e_from = jnp.where(c == 0, pick(l, (0, 3, 1, 3)), pick(h, (0, 2, 3, 1)))
    unit = jnp.concatenate([pick(e_from, (e, ze, gup, gdown)), pick(a_from, (a, za, gup, gdown))], 0)

    def gather(d):
        return lambda x, l, c, y, h: (x + d, l, c, y, h) if c == 0 else (x, l, c, y + d, h)

    order = (0, 1, 3, 2)
    mine = [unit] + [send(unit, gather(d)) for d in order[1:]]
    theirs = [send(value, lambda x, l, c, y, h: (x, l, 1 - c, y, h)) for value in mine]
    at = jnp.stack([c] + [(y - d) % NY * part for d in order] + [(x - d) % NX * part for d in order]).astype(jnp.int32)
    return product(at, mine, theirs, field.shape)


def solution(mesh):
    return jax.shard_map(
        per_device,
        mesh=mesh,
        in_specs=(P(None, "shot", "rcv"),),
        out_specs=P(None, "shot", "rcv"),
        check_vma=False,
    )
```

```python
import jax
import jax.numpy as jnp
from jax import lax
from jax.experimental import pallas as pl
from jax.experimental.pallas import tpu as pltpu
from jax.sharding import PartitionSpec as P

WIDTH = 512
AXES = ("shot", "rcv")
NX, NL, NC, NY, NH = 4, 4, 2, 4, 4
VMEM = pl.BlockSpec(memory_space=pltpu.VMEM)
SMEM = pl.BlockSpec(memory_space=pltpu.SMEM)
HBM = pl.BlockSpec(memory_space=pltpu.HBM)


def moves(rule):
    pairs = []
    for x in range(NX):
        for l in range(NL):
            for c in range(NC):
                for y in range(NY):
                    for h in range(NH):
                        to = rule(x, l, c, y, h)
                        if to is None:
                            continue
                        X, L, C, Y, H = to
                        src = ((x * NL + l) * NC + c) * NY * NH + y * NH + h
                        dst = (((X % NX) * NL + L) * NC + C) * NY * NH + (Y % NY) * NH + H % NH
                        pairs.append((src, dst))
    return pairs


def send(value, rule):
    return lax.ppermute(value, AXES, moves(rule))


def pick(index, choices):
    out = choices[-1]
    for i, choice in enumerate(choices[:-1]):
        out = jnp.where(index == i, choice, out)
    return out


def run(copies):
    for copy in copies:
        copy.start()
    for copy in copies:
        copy.wait()


def first_kernel(role, field, *refs):
    panel, upper, lower, sem = refs[0], refs[1:5], refs[5:9], refs[9]
    rows, cols = upper[0].shape[1:]

    def part(d, t):
        return field.at[:, pl.ds(rows * d, rows), pl.ds(cols * t, cols)]

    @pl.when(role[0] == 1)
    def _():
        run([
            pltpu.make_async_copy(part(d, t), bits[d], sem.at[2 * d + t])
            for d in range(4)
            for t, bits in ((1, upper), (0, lower))
        ])

    @pl.when(role[1] == 1)
    def _():
        run([pltpu.make_async_copy(field.at[:, :, pl.ds(0, cols)], panel, sem.at[8])])

    @pl.when(role[2] == 1)
    def _():
        run([pltpu.make_async_copy(part(d, 0), bit, sem.at[d]) for d, bit in enumerate(upper)])


def first(role, field, shape):
    return pl.pallas_call(
        first_kernel,
        out_shape=[jax.ShapeDtypeStruct((2, field.shape[1], WIDTH), jnp.bfloat16)]
        + [jax.ShapeDtypeStruct(shape, jnp.bfloat16)] * 8,
        in_specs=[SMEM, HBM],
        out_specs=[VMEM] * 9,
        scratch_shapes=[pltpu.SemaphoreType.DMA((9,))],
        compiler_params=pltpu.CompilerParams(vmem_limit_bytes=16 * 1024 * 1024),
    )(role, field)


def second_kernel(role, came, *refs):
    lower, sem = refs[4:8], refs[8]
    rows = lower[0].shape[1]

    @pl.when(role[2] == 1)
    def _():
        run([
            pltpu.make_async_copy(came.at[:, pl.ds(rows * d, rows)], bit, sem.at[d]) for d, bit in enumerate(lower)
        ])


def second(role, came, bits):
    return pl.pallas_call(
        second_kernel,
        out_shape=[jax.ShapeDtypeStruct(bit.shape, bit.dtype) for bit in bits],
        in_specs=[SMEM] + [VMEM] * 5,
        out_specs=[VMEM] * 4,
        input_output_aliases={2 + i: i for i in range(4)},
        scratch_shapes=[pltpu.SemaphoreType.DMA((4,))],
        compiler_params=pltpu.CompilerParams(vmem_limit_bytes=16 * 1024 * 1024),
    )(role, came, *bits)


def product_kernel(at, *refs):
    mine, theirs = refs[0:4], refs[4:8]
    out, lre, lim, buf, sem = refs[8:]
    rows = mine[0].shape[1]
    dot = lambda a, b: jnp.dot(a, b, preferred_element_type=jnp.float32)

    def work(lefts, rights, first):
        copies = []
        for i, left in enumerate(lefts):
            here = pl.ds(rows * i, rows)
            for j in range(4):
                k = pl.ds(pl.multiple_of(at[5 + j], rows), rows)
                re, im = left[first, :, k], left[first + 1, :, k]
                lre[j, here, :rows] = -re
                lre[j, here, rows:] = im
                lim[j, here, :rows] = -im
                lim[j, here, rows:] = -re
            for t in range(2):
                cols = pl.ds(WIDTH * t, WIDTH)
                for q, lhs in ((0, lre), (1, lim)):
                    acc = None
                    for j, right in enumerate(rights):
                        both = right[2 * t : 2 * t + 2].reshape(2 * rows, WIDTH)
                        term = dot(lhs[j, here], both)
                        acc = term if acc is None else acc + term
                    buf[i, q, :, cols] = acc.astype(buf.dtype)
            place = pl.ds(pl.multiple_of(at[1 + i], rows), rows)
            copies.append(pltpu.make_async_copy(buf.at[i], out.at[:, place], sem.at[i]))
            copies[-1].start()
        for copy in copies:
            copy.wait()

    @pl.when(at[0] == 0)
    def _():
        work(theirs, mine, 0)

    @pl.when(at[0] == 1)
    def _():
        work(mine, theirs, 2)


def product(at, mine, theirs, shape):
    rows = mine[0].shape[1]
    return pl.pallas_call(
        product_kernel,
        out_shape=jax.ShapeDtypeStruct(shape, jnp.bfloat16),
        in_specs=[SMEM] + [VMEM] * 8,
        out_specs=HBM,
        scratch_shapes=[
            pltpu.VMEM((4, 4 * rows, 2 * rows), jnp.bfloat16),
            pltpu.VMEM((4, 4 * rows, 2 * rows), jnp.bfloat16),
            pltpu.VMEM((4, 2, rows, shape[2]), jnp.bfloat16),
            pltpu.SemaphoreType.DMA((4,)),
        ],
        compiler_params=pltpu.CompilerParams(vmem_limit_bytes=40 * 1024 * 1024),
        cost_estimate=pl.CostEstimate(flops=8 * shape[1] * shape[2] * WIDTH, bytes_accessed=1 << 22, transcendentals=0),
    )(at, *mine, *theirs)


def per_device(field):
    s, r = lax.axis_index("shot"), lax.axis_index("rcv")
    x, l, c, y, h = s // (NL * NC), s // NC % NL, s % NC, r // NH, r % NH
    part = WIDTH // 4

    left_root = (y == 0) & (h == 0)
    role = jnp.stack([(c == 0) & (x == 0) & (l == 0), left_root & (c == 0), left_root & (c == 1)]).astype(jnp.int32)
    panel, *bits = first(role, field, (2, part, WIDTH))
    upper, lower = bits[:4], bits[4:]
    came = send(panel, lambda x, l, c, y, h: (x, l, 1, y, h) if c == 0 and y == 0 and h == 0 else None)
    lower = second(role, came, lower)

    def scatter(d):
        def rule(x, l, c, y, h):
            if c == 0:
                return (d, l, c, y, h) if x == 0 and l == 0 else None
            return (x, l, c, d, h) if y == 0 and h == 0 else None
        return rule

    at_root = jnp.where(c == 0, x, y) == 0
    a, e = (
        jnp.where(at_root, bits[0], sum(send(bits[d], scatter(d)) for d in (1, 3, 2)))
        for bits in (upper, lower)
    )


    def hop(to):
        def rule(x, l, c, y, h):
            if c == 0:
                return (x, 2, c, y, h) if l == 0 else None
            return (x, l, c, y, to) if h == 0 else None
        return rule

    za, ze = lax.optimization_barrier((send(a, hop(1)), send(e, hop(3))))

    def onwards(step, sources):
        def rule(x, l, c, y, h):
            if c == 0:
                return (x, l + 1, c, y, h) if l in (0, 2) else None
            return (x, l, c, y, h + step) if h in sources else None
        return rule

    start = jnp.where(c == 0, l, h) == 0
    up = jnp.where(start, jnp.where(c == 0, a, e), za)
    down = jnp.where(start, jnp.where(c == 0, e, a), ze)
    up, down = lax.optimization_barrier((up, down))
    gup, gdown = send(up, onwards(1, (0, 1))), send(down, onwards(-1, (0, 3)))
    a_from = jnp.where(c == 0, pick(l, (0, 2, 1, 2)), pick(h, (0, 1, 2, 3)))
    e_from = jnp.where(c == 0, pick(l, (0, 3, 1, 3)), pick(h, (0, 2, 3, 1)))
    unit = jnp.concatenate([pick(e_from, (e, ze, gup, gdown)), pick(a_from, (a, za, gup, gdown))], 0)

    def gather(d):
        return lambda x, l, c, y, h: (x + d, l, c, y, h) if c == 0 else (x, l, c, y + d, h)

    order = (0, 1, 3, 2)
    mine = [unit] + [send(unit, gather(d)) for d in order[1:]]
    theirs = [send(value, lambda x, l, c, y, h: (x, l, 1 - c, y, h)) for value in mine]
    at = jnp.stack([c] + [(y - d) % NY * part for d in order] + [(x - d) % NX * part for d in order]).astype(jnp.int32)
    return product(at, mine, theirs, field.shape)


def solution(mesh):
    return jax.shard_map(
        per_device,
        mesh=mesh,
        in_specs=(P(None, "shot", "rcv"),),
        out_specs=P(None, "shot", "rcv"),
        check_vma=False,
    )
```
